32 devices in a mesh: tile: 4 (over y, x), thick: 8 (over z, core).
Axes of the slice: x: 2, y: 2, z: 4, core: 2. Of those that a mesh axis runs over, the one named last changes fastest.
Arguments:
- concentration: float32 [2, 64, 512, 256], P(None, 'tile', 'thick'), may hold values from 0 to 1
- polymer: float32 [64, 512, 256], P('tile', 'thick'), may hold values from 0.5 to 2
- plates: int32 [256, 6], P('tile'), may hold values from 0 to 511, as said below
Outputs:
- final_conc: float32 [2, 64, 512, 256], P(None, 'tile', 'thick')
The draws below stay inside these ranges and needn't reach their ends.
Inputs may be any that keep to these rules, and one draw needn't show every extreme that they name: `plates`: each row is one platelet; the x length is 1 to 16 and the x range wraps modulo 64; the y and z ranges lie inside the grid. Of the rows held by one device of tile, at most 32 cover cells of any one tile's 16 x positions, and in every draw some tile is covered by exactly 32 rows of every device.
All inputs are finite; a program needn't handle non-finite values.
Results may differ from the reference program's by a relative error of at most 0.0003.
Values sent between devices are 32-bit elements; how exact they have to be, the bound alone decides.
A program may use at most 128 MiB of HBM per device.

```python
import jax
import jax.numpy as jnp
from jax import lax

XT = 16
Y = 256
Z = 512
PL_DEV = 64
STEPS = 2
X = 64
PLATES = 256
N_TILE = 4


def draw_concentration(key, part):
    column = jax.random.uniform(jax.random.fold_in(key, 11), (2, X, 1, Y), jnp.float32)
    cells = jax.random.uniform(jax.random.fold_in(key, 12), (2, X, Z, Y), jnp.float32)
    values = 0.7 * column + 0.3 * cells
    return jnp.clip(values, 0.0, 1.0).astype(jnp.float32)


def draw_polymer(key, part):
    column = jax.random.uniform(jax.random.fold_in(key, 21), (X, 1, Y), jnp.float32)
    cells = jax.random.uniform(jax.random.fold_in(key, 22), (X, Z, Y), jnp.float32)
    mixed = 0.7 * column + 0.3 * cells
    values = 0.5 * jnp.exp(jnp.log(4.0) * mixed)
    return jnp.clip(values, 0.5, 2.0).astype(jnp.float32)


def draw_plates(key, part):
    hot_start = jax.random.randint(jax.random.fold_in(key, 7), (), 0, N_TILE)
    hot_count = PL_DEV // 4
    slot_ids = jnp.arange(PL_DEV, dtype=jnp.int32)
    offsets = jnp.where(slot_ids < hot_count, 0, jnp.where(slot_ids < 2 * hot_count, 1, 2 + (slot_ids - 2 * hot_count) % (N_TILE - 2)))

    def one_source(source):
        subkeys = jax.random.split(jax.random.fold_in(key, 100 + source), 7)
        shuffled = jax.random.permutation(subkeys[0], PL_DEV)
        home_tile = (offsets[shuffled] + hot_start) % N_TILE
        start_x = home_tile * XT + jax.random.randint(subkeys[1], (PL_DEV,), XT // 2, XT)
        length_x = jax.random.randint(subkeys[2], (PL_DEV,), XT // 2 + 1, XT + 1)
        length_y = jax.random.randint(subkeys[3], (PL_DEV,), Y // 8, Y // 4 + 1)
        start_y = jax.random.randint(subkeys[4], (PL_DEV,), 0, Y - length_y + 1)
        length_z = jax.random.randint(subkeys[5], (PL_DEV,), 1, 4)
        start_z = jax.random.randint(subkeys[6], (PL_DEV,), 0, Z - length_z + 1)
        return jnp.stack([start_x, length_x, start_y, length_y, start_z, length_z], axis=1)
    sources = jnp.arange(N_TILE, dtype=jnp.int32)
    return jax.vmap(one_source)(sources).reshape(PLATES, 6).astype(jnp.int32)


def setup_inputs(seed: int = 0) -> dict:
    key_list = jax.random.split(jax.random.key(seed), 4)
    concentration = draw_concentration(jax.random.fold_in(key_list[3], 71), 0)
    polymer = draw_polymer(jax.random.fold_in(key_list[3], 71), 0)
    plates = draw_plates(jax.random.fold_in(key_list[3], 71), 0)
    return dict(concentration=concentration, polymer=polymer, plates=plates)


BLOCKING = 9.0
PLANE_RATE = 0.11
LINE_RATE = 1000.0


def species_column(values):
    return jnp.array(values, dtype=jnp.float32)[:, None, None, None]


def plane_update(centre, minus_x, plus_x, minus_y, plus_y, weight_mx, weight_px, weight_my, weight_py):
    return centre + PLANE_RATE * ((weight_px * (plus_x - centre) - weight_mx * (centre - minus_x)) + (weight_py * (plus_y - centre) - weight_my * (centre - minus_y)))


def coverage(plates, width_x, width_y, width_z):
    pos_x = jnp.arange(width_x, dtype=jnp.int32)
    in_x = (jnp.mod(pos_x[None, :] - plates[:, 0:1], width_x) < plates[:, 1:2]).astype(jnp.float32)
    pos_y = jnp.arange(width_y, dtype=jnp.int32)
    in_y = ((pos_y[None, :] >= plates[:, 2:3]) & (pos_y[None, :] < plates[:, 2:3] + plates[:, 3:4])).astype(jnp.float32)
    pos_z = jnp.arange(width_z, dtype=jnp.int32)
    in_z = ((pos_z[None, :] >= plates[:, 4:5]) & (pos_z[None, :] < plates[:, 4:5] + plates[:, 5:6])).astype(jnp.float32)

    def one_plane(column):
        weights = column[:, None] * in_z
        return jnp.dot(weights.T, in_y, preferred_element_type=jnp.float32)

    return lax.map(one_plane, in_x.T)


def line_solve(right_side, sub_diag, main_diag, super_diag):
    moved_rows = tuple(jnp.moveaxis(array, 2, 0) for array in (right_side, sub_diag, main_diag, super_diag))
    zeros_row = jnp.zeros_like(moved_rows[0][0])

    def forward(carried, row_items):
        prior_factor, prior_state = carried
        rhs_row, sub_row, diag_row, super_row = row_items
        pivot_row = diag_row - sub_row * prior_factor
        factor = super_row / pivot_row
        state_row = (rhs_row - sub_row * prior_state) / pivot_row
        return (factor, state_row), (factor, state_row)

    ignored, (factors, states) = lax.scan(forward, (zeros_row, zeros_row), moved_rows)

    def backward(above_value, row_items):
        factor, state_row = row_items
        solved = state_row - factor * above_value
        return solved, solved

    ignored, values = lax.scan(backward, zeros_row, (factors, states), reverse=True)
    return jnp.moveaxis(values, 0, 2)


def reference(concentration, polymer, plates):
    counted = coverage(plates, X, Y, Z)
    base_diff = polymer / (1.0 + BLOCKING * counted)
    species_ratio = species_column((1.0, 0.6))
    top_level = species_column((1.0, 0.0))
    bottom_level = species_column((0.0, 1.0))
    face_xp = 0.5 * (base_diff + jnp.roll(base_diff, -1, axis=0))
    face_xm = jnp.roll(face_xp, 1, axis=0)
    face_yp = 0.5 * (base_diff + jnp.roll(base_diff, -1, axis=2))
    face_ym = jnp.roll(face_yp, 1, axis=2)
    below_cells = jnp.concatenate([base_diff[:, :1], base_diff[:, :-1]], axis=1)
    above_cells = jnp.concatenate([base_diff[:, 1:], base_diff[:, -1:]], axis=1)
    lower_face = 0.5 * (below_cells + base_diff)
    upper_face = 0.5 * (base_diff + above_cells)
    lower_species = species_ratio * lower_face
    upper_species = species_ratio * upper_face
    sub_diag = -LINE_RATE * lower_species
    super_diag = -LINE_RATE * upper_species
    main_diag = 1.0 + LINE_RATE * (lower_species + upper_species)
    z_index = jnp.arange(Z, dtype=jnp.int32)[:, None]
    edge_term = jnp.where(z_index == 0, LINE_RATE * lower_species * top_level, 0.0) + jnp.where(z_index == Z - 1, LINE_RATE * upper_species * bottom_level, 0.0)
    weight_mx = species_ratio * face_xm
    weight_px = species_ratio * face_xp
    weight_my = species_ratio * face_ym
    weight_py = species_ratio * face_yp
    for step_index in range(STEPS):
        plane = plane_update(concentration, jnp.roll(concentration, 1, axis=1), jnp.roll(concentration, -1, axis=1), jnp.roll(concentration, 1, axis=3), jnp.roll(concentration, -1, axis=3), weight_mx, weight_px, weight_my, weight_py)
        concentration = line_solve(plane + edge_term, sub_diag, main_diag, super_diag)
    return concentration
```

```python
import functools

import jax
import jax.numpy as jnp
from jax import lax
from jax.experimental import pallas as pl
from jax.experimental.pallas import tpu as pltpu
from jax.sharding import PartitionSpec as P

STEPS = 2
BLOCKING = 9.0
PLANE_RATE = 0.11
LINE_RATE = 1000.0
RATIOS = (1.0, 0.6)
F32 = jnp.float32
ROWS = 8
LANES = 128


def kernel(tiles, layers, conc, poly, rec, out, recg, zs, hz, hp, base, ca, cb, rhs,
           inv, low, fac, spike_p, spike_q, val, coef_out, coef_in, red, ends_out, ends_in,
           reply, sides, rec_s, rec_r, zh_s, zh_r, ph_s, ph_r, ch_s, ch_r, co_s, co_r,
           en_s, en_r, re_s, re_r):
    species, rows_x, rows_z, width_y = conc.shape
    halves = width_y // LANES
    groups = rows_x // ROWS
    per = groups * halves
    chunks = species * per
    tile = lax.axis_index("tile")
    layer = lax.axis_index("thick")
    width_x = tiles * rows_x
    every = layers == chunks

    def tile_at(d):
        return lax.rem(tile + d + tiles, tiles)

    def layer_at(d):
        return lax.rem(layer + d + layers, layers)

    def when(cond, fn):
        if every:
            fn()
        else:
            pl.when(cond)(fn)

    def remote(src, dst, send, recv, where):
        return pltpu.make_async_remote_copy(
            src_ref=src, dst_ref=dst, send_sem=send, recv_sem=recv,
            device_id=where, device_id_type=pl.DeviceIdType.MESH)

    barrier = pltpu.get_barrier_semaphore()
    for d in range(1, tiles):
        pl.semaphore_signal(barrier, inc=1, device_id=(tile_at(d), layer),
                            device_id_type=pl.DeviceIdType.MESH)
    for d in range(1, layers):
        pl.semaphore_signal(barrier, inc=1, device_id=(tile, layer_at(d)),
                            device_id_type=pl.DeviceIdType.MESH)

    def copy_plane(x):
        dst = pl.ds(pl.multiple_of((x + 1) * rows_z, rows_z), rows_z)
        for s in range(species):
            for j in range(halves):
                ca[s, j, dst, :] = conc[s, x, :, j * LANES:(j + 1) * LANES]

    copy_plane(0)
    copy_plane(rows_x - 1)
    zs[0] = poly[:, rows_z - 1, :]
    zs[1] = poly[:, 0, :]
    recg[0] = rec[...]
    pl.semaphore_wait(barrier, tiles - 1 + layers - 1)

    pending = []
    rec_copies = [
        remote(rec, recg.at[d], rec_s.at[d], rec_r.at[d], (tile_at(d), layer))
        for d in range(1, tiles)
    ]
    zh_copies = [
        remote(zs.at[0], hz.at[0], zh_s.at[0], zh_r.at[0], (tile, layer_at(1))),
        remote(zs.at[1], hz.at[1], zh_s.at[1], zh_r.at[1], (tile, layer_at(-1))),
    ]
    ph_copies = [
        remote(poly.at[rows_x - 1], hp.at[0], ph_s.at[0], ph_r.at[0], (tile_at(1), layer)),
        remote(poly.at[0], hp.at[1], ph_s.at[1], ph_r.at[1], (tile_at(-1), layer)),
    ]

    def plane_copies(c, step):
        last = pl.ds(rows_x * rows_z, rows_z)
        first = pl.ds(rows_z, rows_z)
        over = pl.ds((rows_x + 1) * rows_z, rows_z)
        under = pl.ds(0, rows_z)
        return [
            remote(c.at[:, :, last, :], c.at[:, :, under, :], ch_s.at[step, 0],
                   ch_r.at[step, 0], (tile_at(1), layer)),
            remote(c.at[:, :, first, :], c.at[:, :, over, :], ch_s.at[step, 1],
                   ch_r.at[step, 1], (tile_at(-1), layer)),
        ]

    ch_copies = plane_copies(ca, 0)
    for copy in rec_copies + zh_copies + ph_copies + ch_copies:
        copy.start()
    pending += rec_copies + zh_copies + ph_copies + ch_copies

    @pl.loop(1, rows_x - 1)
    def _(x):
        copy_plane(x)

    for copy in rec_copies:
        copy.wait_recv()
    table = jnp.concatenate([recg[d] for d in range(tiles)], axis=1)
    total = table.shape[1]
    start_x, len_x = table[0:1], table[1:2]
    start_y, len_y = table[2:3], table[3:4]
    start_z, len_z = table[4:5], table[5:6]

    def wrap(value):
        if width_x & (width_x - 1) == 0:
            return value & (width_x - 1)
        return jnp.mod(value, width_x)

    def inside(pos, start, length):
        return jnp.where((pos >= start) & (pos < start + length), 1.0, 0.0)

    pos_y = lax.broadcasted_iota(jnp.int32, (width_y, total), 0)
    in_y = inside(pos_y, start_y, len_y).astype(jnp.bfloat16)
    pos_z = layer * rows_z + lax.broadcasted_iota(jnp.int32, (rows_z, total), 0)
    in_z = inside(pos_z, start_z, len_z)

    def counted(mask):
        return lax.dot_general(mask.astype(jnp.bfloat16), in_y, (((1,), (1,)), ((), ())),
                               preferred_element_type=F32)

    def put_base(x, polymer):
        in_x = jnp.where(wrap(tile * rows_x + x - start_x) < len_x, 1.0, 0.0)
        values = polymer / (1.0 + BLOCKING * counted(in_z * in_x))
        dst = pl.ds(pl.multiple_of((x + 1) * rows_z, rows_z), rows_z)
        for j in range(halves):
            base[j, dst, :] = values[:, j * LANES:(j + 1) * LANES]

    @pl.loop(0, rows_x)
    def _(x):
        put_base(x, poly[x])

    for copy in zh_copies:
        copy.wait_recv()
    pos_x = tile * rows_x + lax.broadcasted_iota(jnp.int32, (rows_x, total), 0)
    in_x_all = jnp.where(wrap(pos_x - start_x) < len_x, 1.0, 0.0)

    def z_halo(side, z):
        mask = in_x_all * inside(z, start_z, len_z)
        values = hz[side] / (1.0 + BLOCKING * counted(mask))
        return jnp.stack([values[g * ROWS:(g + 1) * ROWS, j * LANES:(j + 1) * LANES]
                          for g in range(groups) for j in range(halves)])

    def base_row(z):
        return jnp.stack([
            base[j, pl.ds((1 + g * ROWS) * rows_z + z, ROWS, stride=rows_z), :]
            for g in range(groups) for j in range(halves)])

    first_base = base_row(0)
    last_base = base_row(rows_z - 1)
    under_base = jnp.where(layer == 0, first_base, z_halo(0, layer * rows_z - 1))
    over_base = jnp.where(layer == layers - 1, last_base, z_halo(1, (layer + 1) * rows_z))

    def factor_row(z, carry, above):
        below, here, prior_f, prior_p = carry
        lower = 0.5 * (below + here)
        upper = 0.5 * (here + above)
        lw = jnp.concatenate([r * lower for r in RATIOS], axis=0)
        up = jnp.concatenate([r * upper for r in RATIOS], axis=0)
        l = -LINE_RATE * lw
        pivot = (1.0 + LINE_RATE * (lw + up)) - l * prior_f
        i = 1.0 / pivot
        f = (-LINE_RATE * up) * i
        li = l * i
        p = -(li * prior_p)
        inv[z] = i
        low[z] = li
        fac[z] = f
        spike_p[z] = p
        return (here, above, f, p)

    shape = (chunks, ROWS, LANES)
    carry = (under_base, first_base, jnp.zeros(shape, F32), jnp.ones(shape, F32))
    carry = lax.fori_loop(0, rows_z - 1, lambda z, c: factor_row(z, c, base_row(z + 1)), carry)
    factor_row(rows_z - 1, carry, over_base)

    unroll = 4

    def spike_rows(n, carry):
        p, q = carry
        for m in range(unroll):
            z = rows_z - 1 - (n * unroll + m)
            f = fac[z]
            p = spike_p[z] - f * p
            q = -(f * q)
            spike_p[z] = p
            spike_q[z] = q
        return p, q

    lax.fori_loop(0, rows_z // unroll, spike_rows, (jnp.zeros(shape, F32), jnp.ones(shape, F32)))

    for member, value in enumerate((spike_p[0], spike_q[0], spike_p[rows_z - 1],
                                    spike_q[rows_z - 1])):
        for c in range(chunks):
            coef_out[c, member] = value[c]

    def to_owner(src, dst, send, recv, d):
        owner = layer_at(d)
        return owner, remote(src.at[owner if every else lax.rem(owner, chunks)], dst.at[layer],
                             send, recv, (tile, owner))

    def send_owned(src, dst, send, recv):
        for d in range(1, layers):
            owner, copy = to_owner(src, dst, send(d), recv(d), d)
            when(owner < chunks, copy.start)

        def keep():
            dst[layer] = src[layer if every else lax.rem(layer, chunks)]

        when(layer < chunks, keep)

    def wait_owned(src, dst, send, recv):
        for d in range(1, layers):
            copy = to_owner(src, dst, send(d), recv(d), d)[1]
            when(layer < chunks, copy.wait_recv)

    def drain_owned(src, dst, send, recv):
        for d in range(1, layers):
            owner, copy = to_owner(src, dst, send(d), recv(d), d)
            when(owner < chunks, copy.wait_send)

    coef_args = (coef_out, coef_in, lambda d: co_s.at[d], lambda d: co_r.at[d])
    send_owned(*coef_args)

    for copy in ph_copies:
        copy.wait_recv()
    put_base(-1, hp[0])
    put_base(rows_x, hp[1])

    lane = lax.broadcasted_iota(jnp.int32, (16, LANES), 1)

    def next_y(parts):
        turned = [pltpu.roll(v, LANES - 1, 1) for v in parts]
        return [jnp.where(lane == LANES - 1, turned[(j + 1) % halves], turned[j])
                for j in range(halves)]

    def prior_y(parts):
        turned = [pltpu.roll(v, 1, 1) for v in parts]
        return [jnp.where(lane == 0, turned[j - 1], turned[j]) for j in range(halves)]

    def plane_x(c, x):
        for z in range(0, rows_z, 16):
            under = pl.ds(pl.multiple_of(x * rows_z, rows_z) + z, 16)
            here = pl.ds(pl.multiple_of((x + 1) * rows_z, rows_z) + z, 16)
            over = pl.ds(pl.multiple_of((x + 2) * rows_z, rows_z) + z, 16)
            b = [base[j, here, :] for j in range(halves)]
            b_next = next_y(b)
            face_xm = [0.5 * (base[j, under, :] + b[j]) for j in range(halves)]
            face_xp = [0.5 * (b[j] + base[j, over, :]) for j in range(halves)]
            face_y = [0.5 * (b[j] + b_next[j]) for j in range(halves)]
            for s in range(species):
                v = [c[s, j, here, :] for j in range(halves)]
                v_next = next_y(v)
                flux = [face_y[j] * (v_next[j] - v[j]) for j in range(halves)]
                back = prior_y(flux)
                for j in range(halves):
                    along = (face_xp[j] * (c[s, j, over, :] - v[j])
                             - face_xm[j] * (v[j] - c[s, j, under, :]))
                    rhs[s, j, under, :] = v[j] + (PLANE_RATE * RATIOS[s]) * (
                        along + (flux[j] - back[j]))

    def strided(ref, z, pad):
        return jnp.stack([
            ref[s, j, pl.ds((pad + g * ROWS) * rows_z + z, ROWS, stride=rows_z), :]
            for s in range(species) for g in range(groups) for j in range(halves)])

    def put_strided(ref, z, pad, value):
        n = 0
        for s in range(species):
            for g in range(groups):
                for j in range(halves):
                    ref[s, j, pl.ds((pad + g * ROWS) * rows_z + z, ROWS, stride=rows_z), :] = value[n]
                    n += 1

    def forward_rows(n, state):
        for m in range(unroll):
            z = n * unroll + m
            state = strided(rhs, z, 0) * inv[z] - low[z] * state
            val[z] = state
        return state

    def backward_rows(n, v):
        for m in range(unroll):
            z = rows_z - 1 - (n * unroll + m)
            v = val[z] - fac[z] * v
            val[z] = v
        return v

    def reduce_matrix():
        wait_owned(*coef_args)
        b = jnp.zeros((ROWS, LANES), F32)
        for k in range(layers):
            red[k, 2] = b
            d = 1.0 / (1.0 - coef_in[k, 0] * b)
            g = coef_in[k, 2] * b * d
            b = coef_in[k, 3] + g * coef_in[k, 1]
            red[k, 0] = d
            red[k, 1] = g

    def reduce_solve(step):
        top = jnp.where(layer < per, 1.0, 0.0)
        a = jnp.full((ROWS, LANES), top, F32)
        prior = []
        heads = []
        for k in range(layers):
            prior.append(a)
            head = ends_in[step, k, 0] + coef_in[k, 0] * a
            heads.append(head)
            a = ends_in[step, k, 1] + coef_in[k, 2] * a + red[k, 1] * head
        f = jnp.full((ROWS, LANES), 1.0 - top, F32)
        for k in range(layers - 1, -1, -1):
            reply[step, k, 1] = f
            f = red[k, 0] * (heads[k] + coef_in[k, 1] * f)
            reply[step, k, 0] = prior[k] + red[k, 2] * f

    def reply_copy(step, d):
        peer = layer_at(d)
        mine = layer if every else lax.rem(layer, chunks)
        return remote(reply.at[step, peer], sides.at[step, mine], re_s.at[step, d],
                      re_r.at[step, d], (tile, peer))

    for step in range(STEPS):
        c_in = ca if step == 0 else cb
        for copy in ch_copies:
            copy.wait_recv()

        @pl.loop(0, rows_x)
        def _(x, c_in=c_in):
            plane_x(c_in, x)

        lax.fori_loop(0, rows_z // unroll, forward_rows, jnp.zeros(shape, F32))
        first = lax.fori_loop(0, rows_z // unroll, backward_rows, jnp.zeros(shape, F32))
        last = val[rows_z - 1]
        for c in range(chunks):
            ends_out[step, c, 0] = first[c]
            ends_out[step, c, 1] = last[c]
        ends_args = (ends_out.at[step], ends_in.at[step],
                     lambda d, step=step: en_s.at[step, d], lambda d, step=step: en_r.at[step, d])
        send_owned(*ends_args)
        if step == 0:
            when(layer < chunks, reduce_matrix)
        wait_owned(*ends_args)

        def answer(step=step):
            reduce_solve(step)
            for d in range(1, layers):
                reply_copy(step, d).start()
            sides[step, layer if every else lax.rem(layer, chunks)] = reply[step, layer]

        when(layer < chunks, answer)
        for d in range(1, layers):
            when(layer_at(-d) < chunks, reply_copy(step, d).wait_recv)
        before = sides[step, :, 0]
        after = sides[step, :, 1]

        def finish_rows(n, carry):
            for m in range(unroll):
                z = n * unroll + m
                put_strided(cb if step + 1 < STEPS else ca, z, 1,
                            val[z] + spike_p[z] * before + spike_q[z] * after)
            return carry

        lax.fori_loop(0, rows_z // unroll, finish_rows, 0)
        if step + 1 < STEPS:
            ch_copies = plane_copies(cb, step + 1)
            for copy in ch_copies:
                copy.start()
            pending += ch_copies
        if step == 0:
            for copy in pending:
                if not any(copy is other for other in ch_copies):
                    copy.wait_send()
            pending = list(ch_copies)
            drain_owned(*coef_args)
        drain_owned(*ends_args)
        for d in range(1, layers):
            when(layer < chunks, reply_copy(step, d).wait_send)

    @pl.loop(0, rows_x)
    def _(x):
        src = pl.ds(pl.multiple_of((x + 1) * rows_z, rows_z), rows_z)
        for s in range(species):
            for j in range(halves):
                out[s, x, :, j * LANES:(j + 1) * LANES] = ca[s, j, src, :]

    for copy in pending:
        copy.wait_send()


def on_device(concentration, polymer, plates):
    species, rows_x, rows_z, width_y = concentration.shape
    tiles = lax.axis_size("tile")
    layers = lax.axis_size("thick")
    halves = width_y // LANES
    chunks = species * (rows_x // ROWS) * halves
    count = plates.shape[0]
    records = jnp.pad(plates.T, ((0, 8 - plates.shape[1]), (0, -count % LANES)))
    line = pltpu.VMEM((rows_z, chunks, ROWS, LANES), F32)
    dma = pltpu.SemaphoreType.DMA
    extended = (halves, (rows_x + 2) * rows_z, LANES)
    scratch = [
        pltpu.VMEM((tiles,) + records.shape, jnp.int32),
        pltpu.VMEM((2, rows_x, width_y), F32),
        pltpu.VMEM((2, rows_x, width_y), F32),
        pltpu.VMEM((2, rows_z, width_y), F32),
        pltpu.VMEM(extended, F32),
        pltpu.VMEM((species,) + extended, F32),
        pltpu.VMEM((species,) + extended, F32),
        pltpu.VMEM((species, halves, rows_x * rows_z, LANES), F32),
        line, line, line, line, line, line,
        pltpu.VMEM((chunks, 4, ROWS, LANES), F32),
        pltpu.VMEM((layers, 4, ROWS, LANES), F32),
        pltpu.VMEM((layers, 3, ROWS, LANES), F32),
        pltpu.VMEM((STEPS, chunks, 2, ROWS, LANES), F32),
        pltpu.VMEM((STEPS, layers, 2, ROWS, LANES), F32),
        pltpu.VMEM((STEPS, layers, 2, ROWS, LANES), F32),
        pltpu.VMEM((STEPS, chunks, 2, ROWS, LANES), F32),
        dma((tiles,)), dma((tiles,)), dma((2,)), dma((2,)), dma((2,)), dma((2,)),
        dma((STEPS, 2)), dma((STEPS, 2)), dma((layers,)), dma((layers,)),
        dma((STEPS, layers)), dma((STEPS, layers)), dma((STEPS, layers)), dma((STEPS, layers)),
    ]
    vmem = pl.BlockSpec(memory_space=pltpu.VMEM)
    return pl.pallas_call(
        functools.partial(kernel, tiles, layers),
        out_shape=jax.ShapeDtypeStruct(concentration.shape, F32),
        in_specs=[vmem, vmem, vmem],
        out_specs=vmem,
        scratch_shapes=scratch,
        compiler_params=pltpu.CompilerParams(
            collective_id=0, has_side_effects=True, vmem_limit_bytes=48 * 2**20),
    )(concentration, polymer, records)


def solution(mesh):
    return jax.shard_map(
        on_device,
        mesh=mesh,
        in_specs=(P(None, "tile", "thick", None), P("tile", "thick", None), P("tile", None)),
        out_specs=P(None, "tile", "thick", None),
        check_vma=False,
    )
```

```python
import functools

import jax
import jax.numpy as jnp
from jax import lax
from jax.experimental import pallas as pl
from jax.experimental.pallas import tpu as pltpu
from jax.sharding import PartitionSpec as P

STEPS = 2
BLOCKING = 9.0
PLANE_RATE = 0.11
LINE_RATE = 1000.0
RATIOS = (1.0, 0.6)
F32 = jnp.float32
ROWS = 8
LANES = 128
PAD = 8


def kernel(tiles, layers, conc, poly_in, rec, out, mine, recg, poly, zs, hz, hp, base, ca, cb, rhs,
           inv, low, fac, spike_p, spike_q, val, coef_out, coef_in, red, ends_out, ends_in,
           reply, sides, rec_s, rec_r, zh_s, zh_r, ph_s, ph_r, ch_s, ch_r, co_s, co_r,
           en_s, en_r, re_s, re_r, in_c, in_p):
    species, rows_x, rows_z, width_y = conc.shape
    halves = width_y // LANES
    groups = rows_x // ROWS
    per = groups * halves
    chunks = species * per
    tile = lax.axis_index("tile")
    layer = lax.axis_index("thick")
    width_x = tiles * rows_x
    pitch = rows_z + PAD
    every = layers == chunks

    def tile_at(d):
        return lax.rem(tile + d + tiles, tiles)

    def layer_at(d):
        return lax.rem(layer + d + layers, layers)

    def when(cond, fn):
        if every:
            fn()
        else:
            pl.when(cond)(fn)

    def remote(src, dst, send, recv, where):
        return pltpu.make_async_remote_copy(
            src_ref=src, dst_ref=dst, send_sem=send, recv_sem=recv,
            device_id=where, device_id_type=pl.DeviceIdType.MESH)

    barrier = pltpu.get_barrier_semaphore()
    for d in range(1, tiles):
        pl.semaphore_signal(barrier, inc=1, device_id=(tile_at(d), layer),
                            device_id_type=pl.DeviceIdType.MESH)
    for d in range(1, layers):
        pl.semaphore_signal(barrier, inc=1, device_id=(tile, layer_at(d)),
                            device_id_type=pl.DeviceIdType.MESH)

    poly_copy = pltpu.make_async_copy(poly_in, poly, in_p)
    poly_copy.start()

    @pl.loop(0, rows_x)
    def _(x):
        dst = pl.ds(pl.multiple_of((x + 1) * pitch, 8), rows_z)
        for s in range(species):
            for j in range(halves):
                pltpu.make_async_copy(conc.at[s, x, :, pl.ds(j * LANES, LANES)],
                                      ca.at[s, j, dst, :], in_c).start()

    mine[...] = jnp.zeros_like(mine)
    mine[0:rec.shape[0], 0:rec.shape[1]] = rec[...]
    recg[0] = mine[...]
    pl.semaphore_wait(barrier, tiles - 1 + layers - 1)

    pending = []
    rec_copies = [
        remote(mine, recg.at[d], rec_s.at[d], rec_r.at[d], (tile_at(d), layer))
        for d in range(1, tiles)
    ]
    zh_copies = [
        remote(zs.at[0], hz.at[0], zh_s.at[0], zh_r.at[0], (tile, layer_at(1))),
        remote(zs.at[1], hz.at[1], zh_s.at[1], zh_r.at[1], (tile, layer_at(-1))),
    ]
    ph_copies = [
        remote(poly_in.at[rows_x - 1], hp.at[0], ph_s.at[0], ph_r.at[0], (tile_at(1), layer)),
        remote(poly_in.at[0], hp.at[1], ph_s.at[1], ph_r.at[1], (tile_at(-1), layer)),
    ]

    def plane_copies(c, step, part):
        span = rows_z // 2
        low_row = part * span
        last = pl.ds(rows_x * pitch + low_row, span)
        first = pl.ds(pitch + low_row, span)
        over = pl.ds((rows_x + 1) * pitch + low_row, span)
        under = pl.ds(low_row, span)
        return [
            remote(c.at[:, :, last, :], c.at[:, :, under, :], ch_s.at[step, part, 0],
                   ch_r.at[step, part, 0], (tile_at(1), layer)),
            remote(c.at[:, :, first, :], c.at[:, :, over, :], ch_s.at[step, part, 1],
                   ch_r.at[step, part, 1], (tile_at(-1), layer)),
        ]

    for copy in rec_copies:
        copy.start()
    poly_copy.wait()
    zs[0] = poly[:, rows_z - 1, :]
    zs[1] = poly[:, 0, :]
    for copy in zh_copies + ph_copies:
        copy.start()
    pltpu.make_async_copy(conc, out, in_c).wait()
    ch_copies = plane_copies(ca, 0, 0) + plane_copies(ca, 0, 1)
    for copy in ch_copies:
        copy.start()
    pending += rec_copies + zh_copies + ph_copies + ch_copies

    for copy in rec_copies:
        copy.wait_recv()
    if 2 * rec.shape[1] == LANES and tiles % 2 == 0:
        table = jnp.concatenate([recg[d] + pltpu.roll(recg[d + 1], LANES // 2, 1)
                                 for d in range(0, tiles, 2)], axis=1)
    else:
        table = jnp.concatenate([recg[d] for d in range(tiles)], axis=1)
    total = table.shape[1]
    start_x, len_x = table[0:1], table[1:2]
    start_y, len_y = table[2:3], table[3:4]
    start_z, len_z = table[4:5], table[5:6]

    def wrap(value):
        if width_x & (width_x - 1) == 0:
            return value & (width_x - 1)
        return jnp.mod(value, width_x)

    def inside(pos, start, length):
        return jnp.where((pos >= start) & (pos < start + length), 1.0, 0.0)

    pos_y = lax.broadcasted_iota(jnp.int32, (width_y, total), 0)
    in_y = inside(pos_y, start_y, len_y).astype(jnp.bfloat16)
    pos_z = layer * rows_z + lax.broadcasted_iota(jnp.int32, (rows_z, total), 0)
    in_z = inside(pos_z, start_z, len_z)

    def counted(mask):
        return lax.dot_general(mask.astype(jnp.bfloat16), in_y, (((1,), (1,)), ((), ())),
                               preferred_element_type=F32)

    def put_base(x, polymer):
        in_x = jnp.where(wrap(tile * rows_x + x - start_x) < len_x, 1.0, 0.0)
        values = polymer / (1.0 + BLOCKING * counted(in_z * in_x))
        dst = pl.ds(pl.multiple_of((x + 1) * pitch, 8), rows_z)
        for j in range(halves):
            base[j, dst, :] = values[:, j * LANES:(j + 1) * LANES]

    @pl.loop(0, rows_x)
    def _(x):
        put_base(x, poly[x])

    for copy in zh_copies:
        copy.wait_recv()
    pos_x = tile * rows_x + lax.broadcasted_iota(jnp.int32, (rows_x, total), 0)
    in_x_all = jnp.where(wrap(pos_x - start_x) < len_x, 1.0, 0.0)

    def z_halo(side, z):
        mask = in_x_all * inside(z, start_z, len_z)
        values = hz[side] / (1.0 + BLOCKING * counted(mask))
        return jnp.stack([values[g * ROWS:(g + 1) * ROWS, j * LANES:(j + 1) * LANES]
                          for g in range(groups) for j in range(halves)])

    def base_row(z):
        return jnp.stack([
            base[j, pl.ds((1 + g * ROWS) * pitch + z, ROWS, stride=pitch), :]
            for g in range(groups) for j in range(halves)])

    first_base = base_row(0)
    last_base = base_row(rows_z - 1)
    under_base = jnp.where(layer == 0, first_base, z_halo(0, layer * rows_z - 1))
    over_base = jnp.where(layer == layers - 1, last_base, z_halo(1, (layer + 1) * rows_z))

    def factor_row(z, carry, above):
        below, here, prior_f, prior_p = carry
        lower = 0.5 * (below + here)
        upper = 0.5 * (here + above)
        lw = jnp.concatenate([r * lower for r in RATIOS], axis=0)
        up = jnp.concatenate([r * upper for r in RATIOS], axis=0)
        l = -LINE_RATE * lw
        pivot = (1.0 + LINE_RATE * (lw + up)) - l * prior_f
        i = 1.0 / pivot
        f = (-LINE_RATE * up) * i
        li = l * i
        p = -(li * prior_p)
        inv[z] = i
        low[z] = li
        fac[z] = f
        spike_p[z] = p
        return (here, above, f, p)

    shape = (chunks, ROWS, LANES)
    carry = (under_base, first_base, jnp.zeros(shape, F32), jnp.ones(shape, F32))
    carry = lax.fori_loop(0, rows_z - 1, lambda z, c: factor_row(z, c, base_row(z + 1)), carry)
    factor_row(rows_z - 1, carry, over_base)

    unroll = 4

    def spike_rows(n, carry):
        p, q = carry
        for m in range(unroll):
            z = rows_z - 1 - (n * unroll + m)
            f = fac[z]
            p = spike_p[z] - f * p
            q = -(f * q)
            spike_p[z] = p
            spike_q[z] = q
        return p, q

    lax.fori_loop(0, rows_z // unroll, spike_rows, (jnp.zeros(shape, F32), jnp.ones(shape, F32)))

    for member, value in enumerate((spike_p[0], spike_q[0], spike_p[rows_z - 1],
                                    spike_q[rows_z - 1])):
        for c in range(chunks):
            coef_out[c, member] = value[c]

    def to_owner(src, dst, send, recv, d):
        owner = layer_at(d)
        return owner, remote(src.at[owner if every else lax.rem(owner, chunks)], dst.at[layer],
                             send, recv, (tile, owner))

    def send_owned(src, dst, send, recv):
        for d in range(1, layers):
            owner, copy = to_owner(src, dst, send(d), recv(d), d)
            when(owner < chunks, copy.start)

        def keep():
            dst[layer] = src[layer if every else lax.rem(layer, chunks)]

        when(layer < chunks, keep)

    def wait_owned(src, dst, send, recv):
        for d in range(1, layers):
            copy = to_owner(src, dst, send(d), recv(d), d)[1]
            when(layer < chunks, copy.wait_recv)

    def drain_owned(src, dst, send, recv):
        for d in range(1, layers):
            owner, copy = to_owner(src, dst, send(d), recv(d), d)
            when(owner < chunks, copy.wait_send)

    coef_args = (coef_out, coef_in, lambda d: co_s.at[d], lambda d: co_r.at[d])
    send_owned(*coef_args)

    for copy in ph_copies:
        copy.wait_recv()
    put_base(-1, hp[0])
    put_base(rows_x, hp[1])

    lane = lax.broadcasted_iota(jnp.int32, (16, LANES), 1)

    def next_y(parts):
        turned = [pltpu.roll(v, LANES - 1, 1) for v in parts]
        return [jnp.where(lane == LANES - 1, turned[(j + 1) % halves], turned[j])
                for j in range(halves)]

    def prior_y(parts):
        turned = [pltpu.roll(v, 1, 1) for v in parts]
        return [jnp.where(lane == 0, turned[j - 1], turned[j]) for j in range(halves)]

    def plane_x(c, x):
        for z in range(0, rows_z, 16):
            under = pl.ds(pl.multiple_of(x * pitch, 8) + z, 16)
            here = pl.ds(pl.multiple_of((x + 1) * pitch, 8) + z, 16)
            over = pl.ds(pl.multiple_of((x + 2) * pitch, 8) + z, 16)
            b = [base[j, here, :] for j in range(halves)]
            b_next = next_y(b)
            face_xm = [0.5 * (base[j, under, :] + b[j]) for j in range(halves)]
            face_xp = [0.5 * (b[j] + base[j, over, :]) for j in range(halves)]
            face_y = [0.5 * (b[j] + b_next[j]) for j in range(halves)]
            for s in range(species):
                v = [c[s, j, here, :] for j in range(halves)]
                v_next = next_y(v)
                flux = [face_y[j] * (v_next[j] - v[j]) for j in range(halves)]
                back = prior_y(flux)
                for j in range(halves):
                    along = (face_xp[j] * (c[s, j, over, :] - v[j])
                             - face_xm[j] * (v[j] - c[s, j, under, :]))
                    rhs[s, j, under, :] = v[j] + (PLANE_RATE * RATIOS[s]) * (
                        along + (flux[j] - back[j]))

    def strided(ref, z, pad):
        return jnp.stack([
            ref[s, j, pl.ds((pad + g * ROWS) * pitch + z, ROWS, stride=pitch), :]
            for s in range(species) for g in range(groups) for j in range(halves)])

    def put_strided(ref, z, pad, value):
        n = 0
        for s in range(species):
            for g in range(groups):
                for j in range(halves):
                    ref[s, j, pl.ds((pad + g * ROWS) * pitch + z, ROWS, stride=pitch), :] = value[n]
                    n += 1

    def forward_rows(n, state):
        for m in range(unroll):
            z = n * unroll + m
            state = strided(rhs, z, 0) * inv[z] - low[z] * state
            val[z] = state
        return state

    def backward_rows(n, v):
        for m in range(unroll):
            z = rows_z - 1 - (n * unroll + m)
            v = val[z] - fac[z] * v
            val[z] = v
        return v

    def reduce_matrix():
        wait_owned(*coef_args)
        b = jnp.zeros((ROWS, LANES), F32)
        for k in range(layers):
            red[k, 2] = b
            d = 1.0 / (1.0 - coef_in[k, 0] * b)
            g = coef_in[k, 2] * b * d
            b = coef_in[k, 3] + g * coef_in[k, 1]
            red[k, 0] = d
            red[k, 1] = g

    def reduce_solve(step):
        top = jnp.where(layer < per, 1.0, 0.0)
        a = jnp.full((ROWS, LANES), top, F32)
        prior = []
        heads = []
        for k in range(layers):
            prior.append(a)
            head = ends_in[step, k, 0] + coef_in[k, 0] * a
            heads.append(head)
            a = ends_in[step, k, 1] + coef_in[k, 2] * a + red[k, 1] * head
        f = jnp.full((ROWS, LANES), 1.0 - top, F32)
        for k in range(layers - 1, -1, -1):
            reply[step, k, 1] = f
            f = red[k, 0] * (heads[k] + coef_in[k, 1] * f)
            reply[step, k, 0] = prior[k] + red[k, 2] * f

    def reply_copy(step, d):
        peer = layer_at(d)
        mine = layer if every else lax.rem(layer, chunks)
        return remote(reply.at[step, peer], sides.at[step, mine], re_s.at[step, d],
                      re_r.at[step, d], (tile, peer))

    for step in range(STEPS):
        c_in = ca if step == 0 else cb

        @pl.loop(1, rows_x - 1)
        def _(x, c_in=c_in):
            plane_x(c_in, x)

        for copy in ch_copies:
            copy.wait_recv()

        @pl.loop(0, 2)
        def _(side, c_in=c_in):
            plane_x(c_in, side * (rows_x - 1))

        lax.fori_loop(0, rows_z // unroll, forward_rows, jnp.zeros(shape, F32))
        first = lax.fori_loop(0, rows_z // unroll, backward_rows, jnp.zeros(shape, F32))
        last = val[rows_z - 1]
        for c in range(chunks):
            ends_out[step, c, 0] = first[c]
            ends_out[step, c, 1] = last[c]
        ends_args = (ends_out.at[step], ends_in.at[step],
                     lambda d, step=step: en_s.at[step, d], lambda d, step=step: en_r.at[step, d])
        send_owned(*ends_args)
        if step == 0:
            when(layer < chunks, reduce_matrix)
        wait_owned(*ends_args)

        def answer(step=step):
            reduce_solve(step)
            for d in range(1, layers):
                reply_copy(step, d).start()
            sides[step, layer if every else lax.rem(layer, chunks)] = reply[step, layer]

        when(layer < chunks, answer)
        for d in range(1, layers):
            when(layer_at(-d) < chunks, reply_copy(step, d).wait_recv)
        before = sides[step, :, 0]
        after = sides[step, :, 1]

        def finish_rows(n, carry):
            for m in range(unroll):
                z = n * unroll + m
                put_strided(cb if step + 1 < STEPS else ca, z, 1,
                            val[z] + spike_p[z] * before + spike_q[z] * after)
            return carry

        half = rows_z // unroll // 2
        sent = []
        for part in range(2):
            lax.fori_loop(part * half, (part + 1) * half, finish_rows, 0)
            if step + 1 < STEPS:
                copies = plane_copies(cb, step + 1, part)
                for copy in copies:
                    copy.start()
                sent += copies
        if step + 1 < STEPS:
            ch_copies = sent
            pending += ch_copies
        if step == 0:
            for copy in pending:
                if not any(copy is other for other in ch_copies):
                    copy.wait_send()
            pending = list(ch_copies)
            drain_owned(*coef_args)
        drain_owned(*ends_args)
        for d in range(1, layers):
            when(layer < chunks, reply_copy(step, d).wait_send)

    @pl.loop(0, rows_x)
    def _(x):
        src = pl.ds(pl.multiple_of((x + 1) * pitch, 8), rows_z)
        for s in range(species):
            for j in range(halves):
                out[s, x, :, j * LANES:(j + 1) * LANES] = ca[s, j, src, :]

    for copy in pending:
        copy.wait_send()


def on_device(concentration, polymer, plates):
    species, rows_x, rows_z, width_y = concentration.shape
    tiles = lax.axis_size("tile")
    layers = lax.axis_size("thick")
    halves = width_y // LANES
    chunks = species * (rows_x // ROWS) * halves
    count = plates.shape[0]
    padded = (8, count + -count % LANES)
    records = plates.T
    line = pltpu.VMEM((rows_z, chunks, ROWS, LANES), F32)
    dma = pltpu.SemaphoreType.DMA
    extended = (halves, (rows_x + 2) * (rows_z + PAD), LANES)
    scratch = [
        pltpu.VMEM(padded, jnp.int32),
        pltpu.VMEM((tiles,) + padded, jnp.int32),
        pltpu.VMEM(polymer.shape, F32),
        pltpu.VMEM((2, rows_x, width_y), F32),
        pltpu.VMEM((2, rows_x, width_y), F32),
        pltpu.VMEM((2, rows_z, width_y), F32),
        pltpu.VMEM(extended, F32),
        pltpu.VMEM((species,) + extended, F32),
        pltpu.VMEM((species,) + extended, F32),
        pltpu.VMEM((species, halves, rows_x * (rows_z + PAD), LANES), F32),
        line, line, line, line, line, line,
        pltpu.VMEM((chunks, 4, ROWS, LANES), F32),
        pltpu.VMEM((layers, 4, ROWS, LANES), F32),
        pltpu.VMEM((layers, 3, ROWS, LANES), F32),
        pltpu.VMEM((STEPS, chunks, 2, ROWS, LANES), F32),
        pltpu.VMEM((STEPS, layers, 2, ROWS, LANES), F32),
        pltpu.VMEM((STEPS, layers, 2, ROWS, LANES), F32),
        pltpu.VMEM((STEPS, chunks, 2, ROWS, LANES), F32),
        dma((tiles,)), dma((tiles,)), dma((2,)), dma((2,)), dma((2,)), dma((2,)),
        dma((STEPS, 2, 2)), dma((STEPS, 2, 2)), dma((layers,)), dma((layers,)),
        dma((STEPS, layers)), dma((STEPS, layers)), dma((STEPS, layers)), dma((STEPS, layers)),
        dma, dma,
    ]
    vmem = pl.BlockSpec(memory_space=pltpu.VMEM)
    hbm = pl.BlockSpec(memory_space=pltpu.HBM)
    return pl.pallas_call(
        functools.partial(kernel, tiles, layers),
        out_shape=jax.ShapeDtypeStruct(concentration.shape, F32),
        in_specs=[hbm, hbm, vmem],
        out_specs=vmem,
        scratch_shapes=scratch,
        compiler_params=pltpu.CompilerParams(
            collective_id=0, has_side_effects=True, vmem_limit_bytes=62 * 2**20),
    )(concentration, polymer, records)


def solution(mesh):
    return jax.shard_map(
        on_device,
        mesh=mesh,
        in_specs=(P(None, "tile", "thick", None), P("tile", "thick", None), P("tile", None)),
        out_specs=P(None, "tile", "thick", None),
        check_vma=False,
    )
```

```python
import functools

import jax
import jax.numpy as jnp
from jax import lax
from jax.experimental import pallas as pl
from jax.experimental.pallas import tpu as pltpu
from jax.sharding import PartitionSpec as P

STEPS = 2
BLOCKING = 9.0
PLANE_RATE = 0.11
LINE_RATE = 1000.0
RATIOS = (1.0, 0.6)
F32 = jnp.float32
ROWS = 8
LANES = 128
PAD = 8


def kernel(tiles, layers, conc, poly_in, rec, out, mine, recg, poly, zs, hz, hp, base, ca, cb, rhs,
           inv, low, fac, spike_p, spike_q, val, coef_out, coef_in, red, ends_out, ends_in,
           reply, sides, rec_s, rec_r, zh_s, zh_r, ph_s, ph_r, ch_s, ch_r, co_s, co_r,
           en_s, en_r, re_s, re_r, in_c, in_p):
    species, rows_x, rows_z, width_y = conc.shape
    halves = width_y // LANES
    groups = rows_x // ROWS
    per = groups * halves
    chunks = species * per
    tile = lax.axis_index("tile")
    layer = lax.axis_index("thick")
    width_x = tiles * rows_x
    pitch = rows_z + PAD
    every = layers == chunks

    def tile_at(d):
        return lax.rem(tile + d + tiles, tiles)

    def layer_at(d):
        return lax.rem(layer + d + layers, layers)

    def when(cond, fn):
        if every:
            fn()
        else:
            pl.when(cond)(fn)

    def when_owner(owner, lo, hi, fn):
        if lo == 0 and hi == chunks:
            when(owner < chunks, fn)
        else:
            pl.when((owner >= lo) & (owner < hi))(fn)

    def remote(src, dst, send, recv, where):
        return pltpu.make_async_remote_copy(
            src_ref=src, dst_ref=dst, send_sem=send, recv_sem=recv,
            device_id=where, device_id_type=pl.DeviceIdType.MESH)

    barrier = pltpu.get_barrier_semaphore()
    for d in range(1, tiles):
        pl.semaphore_signal(barrier, inc=1, device_id=(tile_at(d), layer),
                            device_id_type=pl.DeviceIdType.MESH)
    for d in range(1, layers):
        pl.semaphore_signal(barrier, inc=1, device_id=(tile, layer_at(d)),
                            device_id_type=pl.DeviceIdType.MESH)

    poly_copy = pltpu.make_async_copy(poly_in, poly, in_p)
    poly_copy.start()

    @pl.loop(0, rows_x)
    def _(x):
        dst = pl.ds(pl.multiple_of((x + 1) * pitch, 8), rows_z)
        for s in range(species):
            for j in range(halves):
                pltpu.make_async_copy(conc.at[s, x, :, pl.ds(j * LANES, LANES)],
                                      ca.at[s, j, dst, :], in_c).start()

    mine[...] = jnp.zeros_like(mine)
    mine[0:rec.shape[0], 0:rec.shape[1]] = rec[...]
    recg[0] = mine[...]
    pl.semaphore_wait(barrier, tiles - 1 + layers - 1)

    pending = []
    rec_copies = [
        remote(mine, recg.at[d], rec_s.at[d], rec_r.at[d], (tile_at(d), layer))
        for d in range(1, tiles)
    ]
    zh_copies = [
        remote(zs.at[0], hz.at[0], zh_s.at[0], zh_r.at[0], (tile, layer_at(1))),
        remote(zs.at[1], hz.at[1], zh_s.at[1], zh_r.at[1], (tile, layer_at(-1))),
    ]
    ph_copies = [
        remote(poly_in.at[rows_x - 1], hp.at[0], ph_s.at[0], ph_r.at[0], (tile_at(1), layer)),
        remote(poly_in.at[0], hp.at[1], ph_s.at[1], ph_r.at[1], (tile_at(-1), layer)),
    ]

    def plane_copies(c, step, part):
        last = pl.ds(rows_x * pitch, rows_z)
        first = pl.ds(pitch, rows_z)
        over = pl.ds((rows_x + 1) * pitch, rows_z)
        under = pl.ds(0, rows_z)
        return [
            remote(c.at[part, :, last, :], c.at[part, :, under, :], ch_s.at[step, part, 0],
                   ch_r.at[step, part, 0], (tile_at(1), layer)),
            remote(c.at[part, :, first, :], c.at[part, :, over, :], ch_s.at[step, part, 1],
                   ch_r.at[step, part, 1], (tile_at(-1), layer)),
        ]

    for copy in rec_copies:
        copy.start()
    poly_copy.wait()
    zs[0] = poly[:, rows_z - 1, :]
    zs[1] = poly[:, 0, :]
    for copy in zh_copies + ph_copies:
        copy.start()
    pltpu.make_async_copy(conc, out, in_c).wait()
    ch_copies = plane_copies(ca, 0, 0) + plane_copies(ca, 0, 1)
    for copy in ch_copies:
        copy.start()
    pending += rec_copies + zh_copies + ph_copies + ch_copies

    for copy in rec_copies:
        copy.wait_recv()
    if 2 * rec.shape[1] == LANES and tiles % 2 == 0:
        table = jnp.concatenate([recg[d] + pltpu.roll(recg[d + 1], LANES // 2, 1)
                                 for d in range(0, tiles, 2)], axis=1)
    else:
        table = jnp.concatenate([recg[d] for d in range(tiles)], axis=1)
    total = table.shape[1]
    start_x, len_x = table[0:1], table[1:2]
    start_y, len_y = table[2:3], table[3:4]
    start_z, len_z = table[4:5], table[5:6]

    def wrap(value):
        if width_x & (width_x - 1) == 0:
            return value & (width_x - 1)
        return jnp.mod(value, width_x)

    def inside(pos, start, length):
        return jnp.where((pos >= start) & (pos < start + length), 1.0, 0.0)

    pos_y = lax.broadcasted_iota(jnp.int32, (width_y, total), 0)
    in_y = inside(pos_y, start_y, len_y).astype(jnp.bfloat16)
    pos_z = layer * rows_z + lax.broadcasted_iota(jnp.int32, (rows_z, total), 0)
    in_z = inside(pos_z, start_z, len_z)

    def counted(mask):
        return lax.dot_general(mask.astype(jnp.bfloat16), in_y, (((1,), (1,)), ((), ())),
                               preferred_element_type=F32)

    def put_base(x, polymer):
        in_x = jnp.where(wrap(tile * rows_x + x - start_x) < len_x, 1.0, 0.0)
        values = polymer / (1.0 + BLOCKING * counted(in_z * in_x))
        dst = pl.ds(pl.multiple_of((x + 1) * pitch, 8), rows_z)
        for j in range(halves):
            base[j, dst, :] = values[:, j * LANES:(j + 1) * LANES]

    @pl.loop(0, rows_x)
    def _(x):
        put_base(x, poly[x])

    for copy in zh_copies:
        copy.wait_recv()
    pos_x = tile * rows_x + lax.broadcasted_iota(jnp.int32, (rows_x, total), 0)
    in_x_all = jnp.where(wrap(pos_x - start_x) < len_x, 1.0, 0.0)

    def z_halo(side, z):
        mask = in_x_all * inside(z, start_z, len_z)
        values = hz[side] / (1.0 + BLOCKING * counted(mask))
        return jnp.stack([values[g * ROWS:(g + 1) * ROWS, j * LANES:(j + 1) * LANES]
                          for g in range(groups) for j in range(halves)])

    def base_row(z):
        return jnp.stack([
            base[j, pl.ds((1 + g * ROWS) * pitch + z, ROWS, stride=pitch), :]
            for g in range(groups) for j in range(halves)])

    first_base = base_row(0)
    last_base = base_row(rows_z - 1)
    under_base = jnp.where(layer == 0, first_base, z_halo(0, layer * rows_z - 1))
    over_base = jnp.where(layer == layers - 1, last_base, z_halo(1, (layer + 1) * rows_z))

    def factor_row(z, carry, above):
        below, here, prior_f, prior_p = carry
        lower = 0.5 * (below + here)
        upper = 0.5 * (here + above)
        lw = jnp.concatenate([r * lower for r in RATIOS], axis=0)
        up = jnp.concatenate([r * upper for r in RATIOS], axis=0)
        l = -LINE_RATE * lw
        pivot = (1.0 + LINE_RATE * (lw + up)) - l * prior_f
        i = 1.0 / pivot
        f = (-LINE_RATE * up) * i
        li = l * i
        p = -(li * prior_p)
        inv[z] = i
        low[z] = li
        fac[z] = f
        spike_p[z] = p
        return (here, above, f, p)

    shape = (chunks, ROWS, LANES)
    carry = (under_base, first_base, jnp.zeros(shape, F32), jnp.ones(shape, F32))
    carry = lax.fori_loop(0, rows_z - 1, lambda z, c: factor_row(z, c, base_row(z + 1)), carry)
    factor_row(rows_z - 1, carry, over_base)

    unroll = 4

    def spike_rows(n, carry):
        p, q = carry
        for m in range(unroll):
            z = rows_z - 1 - (n * unroll + m)
            f = fac[z]
            p = spike_p[z] - f * p
            q = -(f * q)
            spike_p[z] = p
            spike_q[z] = q
        return p, q

    lax.fori_loop(0, rows_z // unroll, spike_rows, (jnp.zeros(shape, F32), jnp.ones(shape, F32)))

    for member, value in enumerate((spike_p[0], spike_q[0], spike_p[rows_z - 1],
                                    spike_q[rows_z - 1])):
        for c in range(chunks):
            coef_out[c, member] = value[c]

    def to_owner(src, dst, send, recv, d):
        owner = layer_at(d)
        return owner, remote(src.at[owner if every else lax.rem(owner, chunks)], dst.at[layer],
                             send, recv, (tile, owner))

    def send_owned(src, dst, send, recv, lo=0, hi=chunks):
        for d in range(1, layers):
            owner, copy = to_owner(src, dst, send(d), recv(d), d)
            when_owner(owner, lo, hi, copy.start)

        def keep():
            dst[layer] = src[layer if every else lax.rem(layer, chunks)]

        when_owner(layer, lo, hi, keep)

    def wait_owned(src, dst, send, recv):
        for d in range(1, layers):
            copy = to_owner(src, dst, send(d), recv(d), d)[1]
            when(layer < chunks, copy.wait_recv)

    def drain_owned(src, dst, send, recv):
        for d in range(1, layers):
            owner, copy = to_owner(src, dst, send(d), recv(d), d)
            when(owner < chunks, copy.wait_send)

    coef_args = (coef_out, coef_in, lambda d: co_s.at[d], lambda d: co_r.at[d])
    send_owned(*coef_args)

    for copy in ph_copies:
        copy.wait_recv()
    put_base(-1, hp[0])
    put_base(rows_x, hp[1])

    lane = lax.broadcasted_iota(jnp.int32, (16, LANES), 1)

    def next_y(parts):
        turned = [pltpu.roll(v, LANES - 1, 1) for v in parts]
        return [jnp.where(lane == LANES - 1, turned[(j + 1) % halves], turned[j])
                for j in range(halves)]

    def prior_y(parts):
        turned = [pltpu.roll(v, 1, 1) for v in parts]
        return [jnp.where(lane == 0, turned[j - 1], turned[j]) for j in range(halves)]

    def plane_x(c, x, s):
        for z in range(0, rows_z, 16):
            under = pl.ds(pl.multiple_of(x * pitch, 8) + z, 16)
            here = pl.ds(pl.multiple_of((x + 1) * pitch, 8) + z, 16)
            over = pl.ds(pl.multiple_of((x + 2) * pitch, 8) + z, 16)
            b = [base[j, here, :] for j in range(halves)]
            b_next = next_y(b)
            face_xm = [0.5 * (base[j, under, :] + b[j]) for j in range(halves)]
            face_xp = [0.5 * (b[j] + base[j, over, :]) for j in range(halves)]
            face_y = [0.5 * (b[j] + b_next[j]) for j in range(halves)]
            v = [c[s, j, here, :] for j in range(halves)]
            v_next = next_y(v)
            flux = [face_y[j] * (v_next[j] - v[j]) for j in range(halves)]
            back = prior_y(flux)
            for j in range(halves):
                along = (face_xp[j] * (c[s, j, over, :] - v[j])
                         - face_xm[j] * (v[j] - c[s, j, under, :]))
                rhs[s, j, under, :] = v[j] + (PLANE_RATE * RATIOS[s]) * (
                    along + (flux[j] - back[j]))

    def strided(ref, z, s):
        return jnp.stack([
            ref[s, j, pl.ds(g * ROWS * pitch + z, ROWS, stride=pitch), :]
            for g in range(groups) for j in range(halves)])

    def put_strided(ref, z, s, value):
        for g in range(groups):
            for j in range(halves):
                ref[s, j, pl.ds((1 + g * ROWS) * pitch + z, ROWS, stride=pitch), :] = (
                    value[g * halves + j])

    def forward_rows(s, n, state):
        own = slice(s * per, (s + 1) * per)
        for m in range(unroll):
            z = n * unroll + m
            state = strided(rhs, z, s) * inv[z, own] - low[z, own] * state
            val[z, own] = state
        return state

    def backward_rows(s, n, v):
        own = slice(s * per, (s + 1) * per)
        for m in range(unroll):
            z = rows_z - 1 - (n * unroll + m)
            v = val[z, own] - fac[z, own] * v
            val[z, own] = v
        return v

    def reduce_matrix():
        wait_owned(*coef_args)
        b = jnp.zeros((ROWS, LANES), F32)
        for k in range(layers):
            red[k, 2] = b
            d = 1.0 / (1.0 - coef_in[k, 0] * b)
            g = coef_in[k, 2] * b * d
            b = coef_in[k, 3] + g * coef_in[k, 1]
            red[k, 0] = d
            red[k, 1] = g

    def reduce_solve(step):
        top = jnp.where(layer < per, 1.0, 0.0)
        a = jnp.full((ROWS, LANES), top, F32)
        prior = []
        heads = []
        for k in range(layers):
            prior.append(a)
            head = ends_in[step, k, 0] + coef_in[k, 0] * a
            heads.append(head)
            a = ends_in[step, k, 1] + coef_in[k, 2] * a + red[k, 1] * head
        f = jnp.full((ROWS, LANES), 1.0 - top, F32)
        for k in range(layers - 1, -1, -1):
            reply[step, k, 1] = f
            f = red[k, 0] * (heads[k] + coef_in[k, 1] * f)
            reply[step, k, 0] = prior[k] + red[k, 2] * f

    def reply_copy(step, d):
        peer = layer_at(d)
        mine = layer if every else lax.rem(layer, chunks)
        return remote(reply.at[step, peer], sides.at[step, mine], re_s.at[step, d],
                      re_r.at[step, d], (tile, peer))

    for step in range(STEPS):
        c_in = ca if step == 0 else cb
        ends_args = (ends_out.at[step], ends_in.at[step],
                     lambda d, step=step: en_s.at[step, d], lambda d, step=step: en_r.at[step, d])
        for s in range(species):
            @pl.loop(1, rows_x - 1)
            def _(x, c_in=c_in, s=s):
                plane_x(c_in, x, s)

            for copy in ch_copies[2 * s:2 * s + 2]:
                copy.wait_recv()

            @pl.loop(0, 2)
            def _(side, c_in=c_in, s=s):
                plane_x(c_in, side * (rows_x - 1), s)

            zero = jnp.zeros((per, ROWS, LANES), F32)
            lax.fori_loop(0, rows_z // unroll, functools.partial(forward_rows, s), zero)
            first = lax.fori_loop(0, rows_z // unroll, functools.partial(backward_rows, s), zero)
            for c in range(per):
                ends_out[step, s * per + c, 0] = first[c]
                ends_out[step, s * per + c, 1] = val[rows_z - 1, s * per + c]
            send_owned(*ends_args, s * per, (s + 1) * per)
        if step == 0:
            when(layer < chunks, reduce_matrix)
        wait_owned(*ends_args)

        def answer(step=step):
            reduce_solve(step)
            for d in range(1, layers):
                reply_copy(step, d).start()
            sides[step, layer if every else lax.rem(layer, chunks)] = reply[step, layer]

        when(layer < chunks, answer)
        sent = []
        for s in range(species):
            own = slice(s * per, (s + 1) * per)
            for d in range(1, layers):
                when_owner(layer_at(-d), s * per, (s + 1) * per, reply_copy(step, d).wait_recv)
            before = sides[step, own, 0]
            after = sides[step, own, 1]

            def finish_rows(n, carry, s=s, own=own, before=before, after=after):
                for m in range(unroll):
                    z = n * unroll + m
                    put_strided(cb if step + 1 < STEPS else ca, z, s,
                                val[z, own] + spike_p[z, own] * before + spike_q[z, own] * after)
                return carry

            lax.fori_loop(0, rows_z // unroll, finish_rows, 0)
            if step + 1 < STEPS:
                copies = plane_copies(cb, step + 1, s)
                for copy in copies:
                    copy.start()
                sent += copies
        if step + 1 < STEPS:
            ch_copies = sent
            pending += ch_copies
        if step == 0:
            for copy in pending:
                if not any(copy is other for other in ch_copies):
                    copy.wait_send()
            pending = list(ch_copies)
            drain_owned(*coef_args)
        drain_owned(*ends_args)
        for d in range(1, layers):
            when(layer < chunks, reply_copy(step, d).wait_send)

    @pl.loop(0, rows_x)
    def _(x):
        src = pl.ds(pl.multiple_of((x + 1) * pitch, 8), rows_z)
        for s in range(species):
            for j in range(halves):
                out[s, x, :, j * LANES:(j + 1) * LANES] = ca[s, j, src, :]

    for copy in pending:
        copy.wait_send()


def on_device(concentration, polymer, plates):
    species, rows_x, rows_z, width_y = concentration.shape
    tiles = lax.axis_size("tile")
    layers = lax.axis_size("thick")
    halves = width_y // LANES
    chunks = species * (rows_x // ROWS) * halves
    count = plates.shape[0]
    padded = (8, count + -count % LANES)
    records = plates.T
    line = pltpu.VMEM((rows_z, chunks, ROWS, LANES), F32)
    dma = pltpu.SemaphoreType.DMA
    extended = (halves, (rows_x + 2) * (rows_z + PAD), LANES)
    scratch = [
        pltpu.VMEM(padded, jnp.int32),
        pltpu.VMEM((tiles,) + padded, jnp.int32),
        pltpu.VMEM(polymer.shape, F32),
        pltpu.VMEM((2, rows_x, width_y), F32),
        pltpu.VMEM((2, rows_x, width_y), F32),
        pltpu.VMEM((2, rows_z, width_y), F32),
        pltpu.VMEM(extended, F32),
        pltpu.VMEM((species,) + extended, F32),
        pltpu.VMEM((species,) + extended, F32),
        pltpu.VMEM((species, halves, rows_x * (rows_z + PAD), LANES), F32),
        line, line, line, line, line, line,
        pltpu.VMEM((chunks, 4, ROWS, LANES), F32),
        pltpu.VMEM((layers, 4, ROWS, LANES), F32),
        pltpu.VMEM((layers, 3, ROWS, LANES), F32),
        pltpu.VMEM((STEPS, chunks, 2, ROWS, LANES), F32),
        pltpu.VMEM((STEPS, layers, 2, ROWS, LANES), F32),
        pltpu.VMEM((STEPS, layers, 2, ROWS, LANES), F32),
        pltpu.VMEM((STEPS, chunks, 2, ROWS, LANES), F32),
        dma((tiles,)), dma((tiles,)), dma((2,)), dma((2,)), dma((2,)), dma((2,)),
        dma((STEPS, 2, 2)), dma((STEPS, 2, 2)), dma((layers,)), dma((layers,)),
        dma((STEPS, layers)), dma((STEPS, layers)), dma((STEPS, layers)), dma((STEPS, layers)),
        dma, dma,
    ]
    vmem = pl.BlockSpec(memory_space=pltpu.VMEM)
    hbm = pl.BlockSpec(memory_space=pltpu.HBM)
    return pl.pallas_call(
        functools.partial(kernel, tiles, layers),
        out_shape=jax.ShapeDtypeStruct(concentration.shape, F32),
        in_specs=[hbm, hbm, vmem],
        out_specs=vmem,
        scratch_shapes=scratch,
        compiler_params=pltpu.CompilerParams(
            collective_id=0, has_side_effects=True, vmem_limit_bytes=62 * 2**20),
    )(concentration, polymer, records)


def solution(mesh):
    return jax.shard_map(
        on_device,
        mesh=mesh,
        in_specs=(P(None, "tile", "thick", None), P("tile", "thick", None), P("tile", None)),
        out_specs=P(None, "tile", "thick", None),
        check_vma=False,
    )
```
